1024 devices in a mesh: row: 64 (over y, x, z_hi), col: 16 (over z_lo, core).
Axes of the slice: x: 4, y: 8, z: 16 (z_hi: 2, z_lo: 8; z = z_hi * 8 + z_lo), core: 2. Of those that a mesh axis runs over, the one named last changes fastest.
Arguments:
- a_blocks: bfloat16 [256, 64, 128, 128], P('row', 'col'), may hold values from -6 to 6
- a_rows: int32 [256, 64], P('row', 'col'), may hold values from 0 to 1
- a_count: int32 [256, 16], P('row', 'col'), may hold values from 0 to 4
- b_blocks: bfloat16 [128, 64, 128, 128], P('row', 'col'), may hold values from -0.5 to 0.5
- b_cols: int32 [128, 64], P('row', 'col'), may hold values from 0 to 1
- b_count: int32 [128, 16], P('row', 'col'), may hold values from 0 to 4
- c_keep: int32 [128, 32], P('row', 'col'), may hold values 0 or 1
Outputs:
- c_blocks: float32 [128, 32, 128, 128], P('row', 'col')
The draws below stay inside these ranges and needn't reach their ends.
Inputs may be any that keep to these rules, and one draw needn't show every extreme that they name: `a_count`: some block columns of some A piece are full in every draw. `b_count`: some block rows of some B piece are full in every draw.
All inputs are finite; a program needn't handle non-finite values. No bound on the sum of `c_keep` on one device may be relied on, other than what follows from the above.
Results may differ from the reference program's by a relative error of at most 0.0003.
Values may be sent and summed in bfloat16 or wider, within the bound.
No kernel may reach another device: no remote copies, remote signals or barrier semaphores. Data moves between devices by JAX's collectives and lax.ppermute only.
A program may use at most 32 MiB of HBM per device.

```python
import jax
import jax.numpy as jnp
from jax import lax

BS = 128
KB = 2
D = 4
RB = 2
SECTIONS = 8
AROWS = 256
KROWS = 128
SCOLS = 64
CROWS = 128
CCOLS = 32
N_ROW = 64
N_COL = 16


def with_ends(values, rng, smallest, top_value):
    longest = values.shape.index(max(values.shape))
    spots = []
    for shift in (0, 1):
        where = [jax.random.randint(jax.random.fold_in(rng, axis), (), 0, length) for axis, length in enumerate(values.shape)]
        where[longest] = (where[longest] + shift) % values.shape[longest]
        spots.append(tuple(where))
    return values.at[spots[0]].set(smallest).at[spots[1]].set(top_value)


def block_levels(own_key, extent, cuts, smallest, top_value):
    gain = 1.0
    for dim, shards_of in cuts:
        heights = jax.random.uniform(jax.random.fold_in(jax.random.fold_in(own_key, 6), dim), (shards_of,), jnp.float32, smallest / len(cuts), top_value / len(cuts))
        gain = gain * jnp.repeat(jnp.exp(heights), extent[dim] // shards_of).reshape((-1,) + (1,) * (len(extent) - 1 - dim))
    return gain


def normal_values(rng, shape, scale, bound, pieces=(), kind=jnp.bfloat16):
    entries = scale * jax.random.normal(rng, shape, jnp.float32)
    if pieces:
        entries = entries * block_levels(rng, shape, pieces, -0.22, 0.18)
    return jnp.clip(entries, -bound, bound).astype(kind)


def setup_inputs(seed: int = 0) -> dict:
    keys = jax.random.split(jax.random.key(seed), 8)
    return {
        "a_blocks": normal_values(keys[0], (AROWS, SCOLS, BS, BS), 1.0, 6.0, ((0, 64), (1, 16))),
        "a_rows": with_ends(jax.random.randint(keys[1], (AROWS, SCOLS), 0, RB), jax.random.fold_in(keys[1], 1), 0, RB - 1).astype(jnp.int32),
        "a_count": with_ends(jax.random.randint(keys[2], (AROWS, N_COL), 0, D + 1), jax.random.fold_in(keys[2], 1), 0, D).astype(jnp.int32),
        "b_blocks": normal_values(keys[3], (KROWS, SCOLS, BS, BS), BS ** -0.5, 0.5, ((0, 64), (1, 16))),
        "b_cols": with_ends(jax.random.randint(keys[4], (KROWS, SCOLS), 0, RB), jax.random.fold_in(keys[4], 1), 0, RB - 1).astype(jnp.int32),
        "b_count": with_ends(jax.random.randint(keys[5], (KROWS, N_COL), 0, D + 1), jax.random.fold_in(keys[5], 1), 0, D).astype(jnp.int32),
        "c_keep": with_ends((jax.random.randint(keys[6], (CROWS, CCOLS), 0, 3) < 1).astype(jnp.int32), jax.random.fold_in(keys[6], 1), 0, 1),
    }


def section_product(a_tiles, a_which, a_many, b_tiles, b_which, b_many):
    slot_ids = lax.broadcasted_iota(jnp.int32, a_which.shape, 1)
    a_live = slot_ids < a_many
    b_live = slot_ids < b_many
    picks = jnp.arange(RB, dtype=jnp.int32)
    row_hits = jnp.where((a_which[:, :, None] == picks) & a_live[:, :, None], 1.0, 0.0).astype(jnp.float32)
    col_hits = jnp.where((b_which[:, :, None] == picks) & b_live[:, :, None], 1.0, 0.0).astype(jnp.float32)
    products = jnp.einsum("kdxy,keyz->kdexz", a_tiles.astype(jnp.float32), b_tiles.astype(jnp.float32), precision=lax.Precision.HIGHEST)
    weight = jnp.einsum("kdi,kej->ijkde", row_hits, col_hits, precision=lax.Precision.HIGHEST).reshape(RB * RB, -1)
    placed = jnp.dot(weight, products.reshape(weight.shape[1], -1), precision=lax.Precision.HIGHEST)
    return placed.reshape(RB, RB, BS, BS)


def reference(a_blocks, a_rows, a_count, b_blocks, b_cols, b_count, c_keep):
    a_grid = a_blocks.reshape(N_ROW, 2, KB, N_COL, D, BS, BS).transpose(0, 3, 1, 2, 4, 5, 6)
    a_index = a_rows.reshape(N_ROW, 2, KB, N_COL, D).transpose(0, 3, 1, 2, 4)
    a_fill = a_count.reshape(N_ROW, 2, KB, N_COL, 1).transpose(0, 3, 1, 2, 4)
    b_grid = b_blocks.reshape(N_ROW, KB, N_COL, D, BS, BS).transpose(0, 2, 1, 3, 4, 5)
    b_index = b_cols.reshape(N_ROW, KB, N_COL, D).transpose(0, 2, 1, 3)
    b_fill = b_count.reshape(N_ROW, KB, N_COL, 1).transpose(0, 2, 1, 3)

    def one_tile(device_id):
        row_at = device_id // N_COL
        col_at = device_id % N_COL
        summed = jnp.zeros((RB, RB, BS, BS), jnp.float32)
        for section_at in range(SECTIONS):
            a_col = (col_at + section_at) % N_COL
            half = (col_at + section_at) // N_COL
            b_row = (row_at + section_at) % N_ROW
            summed = summed + section_product(a_grid[row_at, a_col, half], a_index[row_at, a_col, half], a_fill[row_at, a_col, half], b_grid[b_row, col_at], b_index[b_row, col_at], b_fill[b_row, col_at])
        return summed

    tiles = lax.map(one_tile, jnp.arange(N_ROW * N_COL, dtype=jnp.int32))
    tiles = tiles.reshape(N_ROW, N_COL, RB, RB, BS, BS).transpose(0, 2, 1, 3, 4, 5).reshape(N_ROW * RB, N_COL * RB, BS, BS)
    return jnp.where(c_keep[:, :, None, None] == 1, tiles, jnp.zeros_like(tiles))
```

```python
import functools

import jax
import jax.numpy as jnp
from jax import lax
from jax.experimental import pallas as pl
from jax.experimental.pallas import tpu as pltpu
from jax.sharding import PartitionSpec as P

BS = 128
VALUES = 4 * BS
ROWS = VALUES + 16
STEPS = 16.0
TOP = 32767.0
FLOOR = 2.0**-100


def level_of(biggest):
    return jnp.ceil(STEPS * jnp.log2(jnp.maximum(biggest, FLOOR))) + 1.0


def coded(values, level):
    scaled = values * (TOP * jnp.exp2(level * (-1.0 / STEPS)))
    return jnp.round(scaled).astype(jnp.int32).astype(jnp.int16)


def slot_sum(blocks, which, many, row, target):
    total = jnp.zeros((BS, BS), jnp.float32)
    live = many[row, 0]
    for d in range(4):
        hit = jnp.logical_and(d < live, which[row, d] == target)
        total = total + blocks[row, d].astype(jnp.float32) * jnp.where(hit, 1.0, 0.0)
    return total


def level_rows(levels):
    at = lax.broadcasted_iota(jnp.int32, (16, BS), 0)
    rows = jnp.zeros((16, BS), jnp.float32)
    for n, level in enumerate(levels):
        rows = jnp.where(at == n, level, rows)
    return rows.astype(jnp.int32).astype(jnp.int16)


def pack_b(which, many, blocks, out):
    levels = []
    for k in range(2):
        sums = [slot_sum(blocks, which, many, k, j) for j in range(2)]
        biggest = jnp.max(jnp.maximum(jnp.abs(sums[0]), jnp.abs(sums[1])), axis=1, keepdims=True)
        level = level_of(biggest)
        for j in range(2):
            out[pl.ds((2 * k + j) * BS, BS), :] = coded(sums[j], level)
        levels.append(jnp.transpose(jnp.broadcast_to(level, (BS, BS)))[0:1, :])
    out[pl.ds(VALUES, 16), :] = level_rows(levels)


def pack_a(which, many, half, blocks, own, sent):
    def one(first, out):
        levels = []
        for k in range(2):
            for i in range(2):
                total = slot_sum(blocks, which, many, first + k, i)
                level = level_of(jnp.max(jnp.abs(total), axis=0, keepdims=True))
                out[pl.ds((2 * k + i) * BS, BS), :] = coded(total, level)
                levels.append(level)
        out[pl.ds(VALUES, 16), :] = level_rows(levels)

    one(0, own)

    @pl.when(half[0] == 0)
    def _():
        sent[...] = own[...]

    @pl.when(half[0] == 1)
    def _():
        one(2, sent)


SMEM = pl.BlockSpec(memory_space=pltpu.SMEM)
VMEM = pl.BlockSpec(memory_space=pltpu.VMEM)
PIECE = jax.ShapeDtypeStruct((ROWS, BS), jnp.int16)


def packed_b(blocks, which, many):
    return pl.pallas_call(
        pack_b,
        out_shape=PIECE,
        in_specs=[SMEM, SMEM, VMEM],
        out_specs=VMEM,
        name="pack_b",
        cost_estimate=pl.CostEstimate(flops=2_000_000, bytes_accessed=400_000, transcendentals=0),
    )(which, many, blocks)


def packed_a(blocks, which, many, half):
    return pl.pallas_call(
        pack_a,
        out_shape=(PIECE, PIECE),
        in_specs=[SMEM, SMEM, SMEM, VMEM],
        out_specs=(VMEM, VMEM),
        name="pack_a",
        cost_estimate=pl.CostEstimate(flops=4_000_000, bytes_accessed=800_000, transcendentals=0),
    )(which, many, half, blocks)


def two_parts(x):
    high = x.astype(jnp.bfloat16)
    return high, (x - high.astype(jnp.float32)).astype(jnp.bfloat16)


def section(a, b):
    a_levels = a[pl.ds(VALUES, 16), :].astype(jnp.int32).astype(jnp.float32)
    b_levels = b[pl.ds(VALUES, 16), :].astype(jnp.int32).astype(jnp.float32)
    a_scales = jnp.exp2(a_levels * (1.0 / STEPS))
    b_scales = jnp.exp2(b_levels * (1.0 / STEPS))
    lefts = []
    rights = []
    for k in range(2):
        tall = []
        wide = []
        for i in range(2):
            v = a[pl.ds((2 * k + i) * BS, BS), :].astype(jnp.int32).astype(jnp.float32)
            n = 2 * k + i
            tall.append((v * (1.0 / TOP)) * a_scales[n : n + 1, :] * b_scales[k : k + 1, :])
            wide.append(b[pl.ds(n * BS, BS), :].astype(jnp.int32).astype(jnp.float32))
        lefts.append(jnp.concatenate(tall, axis=0))
        rights.append(jnp.concatenate(wide, axis=1))
    a_high, a_low = two_parts(jnp.concatenate(lefts, axis=1))
    b_high, b_low = two_parts(jnp.concatenate(rights, axis=0))
    dot = functools.partial(jnp.dot, preferred_element_type=jnp.float32)
    return dot(a_high, b_high) + (dot(a_high, b_low) + dot(a_low, b_high))


def final(keep, a0, a1, a2, a3, others, b0, b1, b2, b3, c0, c1, c2, c3, out):
    total = jnp.zeros((2 * BS, 2 * BS), jnp.float32)
    for t, (a, b, c) in enumerate(zip((a0, a1, a2, a3), (b0, b1, b2, b3), (c0, c1, c2, c3))):
        total = total + section(a, b) + section(others.at[t], c)
    total = total * (1.0 / TOP)
    for i in range(2):
        for j in range(2):
            kept = keep[i, j] == 1
            out[i, j] = jnp.where(kept, total[i * BS : (i + 1) * BS, j * BS : (j + 1) * BS], 0.0)


def finished(keep, *pieces):
    return pl.pallas_call(
        final,
        out_shape=jax.ShapeDtypeStruct((2, 2, BS, BS), jnp.float32),
        in_specs=[SMEM] + [VMEM] * 13,
        out_specs=VMEM,
        name="final",
        cost_estimate=pl.CostEstimate(flops=800_000_000, bytes_accessed=2_500_000, transcendentals=0),
        compiler_params=pltpu.CompilerParams(vmem_limit_bytes=32 << 20),
    )(keep, *pieces)


def moved(x, rows, cols, goal, takes_part=None):
    pairs = []
    for p in range(rows):
        for q in range(cols):
            if takes_part is None or takes_part(p, q):
                to_p, to_q = goal(p, q)
                pairs.append((p * cols + q, (to_p % rows) * cols + to_q % cols))
    return lax.ppermute(x, ("row", "col"), pairs)


def low_plane(p, q):
    return p % 2 == 0


def high_plane(p, q):
    return p % 2 == 1


def per_device(a_blocks, a_rows, a_count, b_blocks, b_cols, b_count, c_keep):
    rows = lax.axis_size("row")
    cols = lax.axis_size("col")
    go = functools.partial(moved, rows=rows, cols=cols)
    col_at = lax.axis_index("col")
    chip = col_at // 2
    core = col_at % 2
    in_quad = chip % 4

    b_own = packed_b(b_blocks, b_cols, b_count)
    b_next_low = go(b_own, goal=lambda p, q: (p - 1, q), takes_part=high_plane)
    half = jnp.where(chip < 4, 1, 0).astype(jnp.int32).reshape(1)
    a_own, a_sent = packed_a(a_blocks, a_rows, a_count, half)

    def swap_goal(p, q):
        return p, q ^ 8

    def quad_goal(t):
        return lambda p, q: (p, q // 8 * 8 + (q % 8 - 2 * t) % 8)

    a_far = go(a_sent, goal=swap_goal)
    b_same = [go(b_own, goal=lambda p, q, t=t: (p - 2 * t, q)) for t in (1, 2, 3)]
    a_same = []
    for t in (1, 2, 3):
        a_same.append(go(jnp.where(in_quad < t, a_far, a_own), goal=quad_goal(t)))
    b_next_high = go(b_own, goal=lambda p, q: (p - 1, q), takes_part=low_plane)
    b_next = jnp.where(lax.axis_index("row") % 2 == 0, b_next_low, b_next_high)
    b_other = [go(b_next, goal=lambda p, q, t=t: (p - 2 * t, q)) for t in (1, 2, 3)]
    mine = [a_own] + a_same
    give = jnp.where(core == 0, jnp.stack(mine[1:] + [a_far]), jnp.stack(mine))
    others = go(give, goal=lambda p, q: (p, q ^ 1))
    return finished(c_keep, *mine, others, b_own, *b_same, b_next, *b_other)


def solution(mesh):
    placed = (
        P("row", "col", None, None),
        P("row", "col"),
        P("row", "col"),
        P("row", "col", None, None),
        P("row", "col"),
        P("row", "col"),
        P("row", "col"),
    )
    return jax.shard_map(
        per_device,
        mesh=mesh,
        in_specs=placed,
        out_specs=P("row", "col", None, None),
        check_vma=False,
    )
```

```python
import functools

import jax
import jax.numpy as jnp
from jax import lax
from jax.experimental import pallas as pl
from jax.experimental.pallas import tpu as pltpu
from jax.sharding import PartitionSpec as P

BS = 128
VALUES = 4 * BS
ROWS = VALUES + 16
STEPS = 16.0
TOP = 32767.0
FLOOR = 2.0**-100


def level_of(biggest):
    return jnp.ceil(STEPS * jnp.log2(jnp.maximum(biggest, FLOOR))) + 1.0


def coded(values, level):
    scaled = values * (TOP * jnp.exp2(level * (-1.0 / STEPS)))
    return jnp.round(scaled).astype(jnp.int32).astype(jnp.int16)


def slot_sum(blocks, which, many, row, target):
    total = jnp.zeros((BS, BS), jnp.float32)
    live = many[0, row]
    for d in range(4):
        hit = jnp.logical_and(d < live, which[row, d] == target)
        total = total + blocks[row, d].astype(jnp.float32) * jnp.where(hit, 1.0, 0.0)
    return total


def level_rows(levels):
    at = lax.broadcasted_iota(jnp.int32, (16, BS), 0)
    rows = jnp.zeros((16, BS), jnp.float32)
    for n, level in enumerate(levels):
        rows = jnp.where(at == n, level, rows)
    return rows.astype(jnp.int32).astype(jnp.int16)


def pack_b(which, many, blocks, out):
    levels = []
    for k in range(2):
        sums = [slot_sum(blocks, which, many, k, j) for j in range(2)]
        biggest = jnp.max(jnp.maximum(jnp.abs(sums[0]), jnp.abs(sums[1])), axis=1, keepdims=True)
        level = level_of(biggest)
        for j in range(2):
            out[pl.ds((2 * k + j) * BS, BS), :] = coded(sums[j], level)
        levels.append(jnp.transpose(jnp.broadcast_to(level, (BS, BS)))[0:1, :])
    out[pl.ds(VALUES, 16), :] = level_rows(levels)


def pack_a(which, many, chip, blocks, own, sent):
    def one(first, out):
        levels = []
        for k in range(2):
            for i in range(2):
                total = slot_sum(blocks, which, many, first + k, i)
                level = level_of(jnp.max(jnp.abs(total), axis=0, keepdims=True))
                out[pl.ds((2 * k + i) * BS, BS), :] = coded(total, level)
                levels.append(level)
        out[pl.ds(VALUES, 16), :] = level_rows(levels)

    one(0, own)

    @pl.when(chip[0] < 4)
    def _():
        one(2, sent)

    @pl.when(chip[0] >= 4)
    def _():
        sent[...] = own[...]


SMEM = pl.BlockSpec(memory_space=pltpu.SMEM)
VMEM = pl.BlockSpec(memory_space=pltpu.VMEM)
PIECE = jax.ShapeDtypeStruct((ROWS, BS), jnp.int16)


def packed_b(blocks, which, many):
    return pl.pallas_call(
        pack_b,
        out_shape=PIECE,
        in_specs=[SMEM, SMEM, VMEM],
        out_specs=VMEM,
        name="pack_b",
        cost_estimate=pl.CostEstimate(flops=2_000_000, bytes_accessed=400_000, transcendentals=0),
    )(which, many, blocks)


def packed_a(blocks, which, many, chip):
    return pl.pallas_call(
        pack_a,
        out_shape=(PIECE,) * 2,
        in_specs=[SMEM, SMEM, SMEM, VMEM],
        out_specs=(VMEM,) * 2,
        name="pack_a",
        cost_estimate=pl.CostEstimate(flops=4_000_000, bytes_accessed=800_000, transcendentals=0),
    )(which, many, chip, blocks)


def two_parts(x):
    high = x.astype(jnp.bfloat16)
    return high, (x - high.astype(jnp.float32)).astype(jnp.bfloat16)


def section(a, b):
    a_levels = a[pl.ds(VALUES, 16), :].astype(jnp.int32).astype(jnp.float32)
    b_levels = b[pl.ds(VALUES, 16), :].astype(jnp.int32).astype(jnp.float32)
    a_scales = jnp.exp2(a_levels * (1.0 / STEPS))
    b_scales = jnp.exp2(b_levels * (1.0 / STEPS))
    lefts = []
    rights = []
    for k in range(2):
        tall = []
        wide = []
        for i in range(2):
            v = a[pl.ds((2 * k + i) * BS, BS), :].astype(jnp.int32).astype(jnp.float32)
            n = 2 * k + i
            tall.append((v * (1.0 / TOP)) * a_scales[n : n + 1, :] * b_scales[k : k + 1, :])
            wide.append(b[pl.ds(n * BS, BS), :].astype(jnp.int32).astype(jnp.float32))
        lefts.append(jnp.concatenate(tall, axis=0))
        rights.append(jnp.concatenate(wide, axis=1))
    a_high, a_low = two_parts(jnp.concatenate(lefts, axis=1))
    b_high, b_low = two_parts(jnp.concatenate(rights, axis=0))
    dot = functools.partial(jnp.dot, preferred_element_type=jnp.float32)
    return dot(a_high, b_high) + (dot(a_high, b_low) + dot(a_low, b_high))


def kept(keep, total, out):
    for i in range(2):
        for j in range(2):
            block = total[i * BS : (i + 1) * BS, j * BS : (j + 1) * BS] * (1.0 / TOP)
            out[i, j] = jnp.where(keep[i, j] == 1, block, 0.0)


def slots_of(spot):
    chip, core = spot[0], spot[1]
    return [lax.rem(chip + t, 4) for t in range(4)], [lax.rem(chip + core + t, 4) for t in range(4)]


def kept(keep, total, out):
    for i in range(2):
        for j in range(2):
            block = total[i * BS : (i + 1) * BS, j * BS : (j + 1) * BS] * (1.0 / TOP)
            out[i, j] = jnp.where(keep[i, j] == 1, block, 0.0)


def final(spot, keep, mine, others, z0, z1, z2, z3, out):
    total = jnp.zeros((2 * BS, 2 * BS), jnp.float32)
    for s, t, z in zip(*slots_of(spot), (z0, z1, z2, z3)):
        total = total + section(mine.at[s], z.at[0]) + section(others.at[t], z.at[1])
    kept(keep, total, out)


def summed(body, keep, *pieces):
    return pl.pallas_call(
        body,
        out_shape=jax.ShapeDtypeStruct((2, 2, BS, BS), jnp.float32),
        in_specs=[SMEM] * len(keep) + [VMEM] * len(pieces),
        out_specs=VMEM,
        name=body.__name__,
        cost_estimate=pl.CostEstimate(flops=800_000_000, bytes_accessed=2_500_000, transcendentals=0),
        compiler_params=pltpu.CompilerParams(vmem_limit_bytes=32 << 20),
    )(*keep, *pieces)


def moved(x, rows, cols, goal, takes_part=None):
    pairs = []
    for p in range(rows):
        for q in range(cols):
            if takes_part is None or takes_part(p, q):
                to_p, to_q = goal(p, q)
                pairs.append((p * cols + q, (to_p % rows) * cols + to_q % cols))
    return lax.ppermute(x, ("row", "col"), pairs)


def low_plane(p, q):
    return p % 2 == 0


def high_plane(p, q):
    return p % 2 == 1


def per_device(a_blocks, a_rows, a_count, b_blocks, b_cols, b_count, c_keep):
    rows = lax.axis_size("row")
    cols = lax.axis_size("col")
    go = functools.partial(moved, rows=rows, cols=cols)
    col_at = lax.axis_index("col")
    chip = col_at // 2
    core = col_at % 2

    on_low = lax.axis_index("row") % 2 == 0
    chip_at = chip.astype(jnp.int32).reshape(1)
    in_quad = chip % 4
    spot = jnp.stack([in_quad, core]).astype(jnp.int32)
    back = lambda p, q: (p - 1, q)

    def spread(x, t, plane):
        return go(x, goal=lambda p, q: (p - 2 * t, q), takes_part=plane)

    def after(x, done):
        return lax.optimization_barrier((x, done))[0]

    slot = lax.broadcasted_iota(jnp.int32, (4, 1, 1), 0)
    quads = [[8 * h + 2 * j + c for j in range(4)] for h in range(cols // 8) for c in range(2)]

    def far_half(plane, blocks):
        a_own, a_sent = packed_a(blocks, a_rows, a_count.T, chip_at)
        a_far = go(a_sent, goal=lambda p, q: (p, q ^ 8), takes_part=plane)
        return jnp.where(slot <= in_quad, a_own[None], a_far[None]), a_far

    def nothing():
        return jnp.zeros((4, *PIECE.shape), PIECE.dtype), jnp.zeros(PIECE.shape, PIECE.dtype)

    def shared(plane, b_own, b_next, give, a_far):
        mine = lax.all_to_all(give, "col", 0, 0, axis_index_groups=quads)
        pair = jnp.stack([b_own, b_next])
        pairs = [pair] + [spread(pair, t, plane) for t in (1, 2, 3)]
        own_slot = jnp.logical_and(slot == in_quad, core == 0)
        given = jnp.where(own_slot, a_far[None], after(mine, pairs))
        others = go(given, goal=lambda p, q: (p, q ^ 1), takes_part=plane)
        return summed(final, [spot, c_keep], mine, others, *pairs)

    b_own = packed_b(b_blocks, b_cols, b_count.T)
    b_next_low = go(b_own, goal=back, takes_part=high_plane)
    blocks = after(a_blocks, b_own)
    low_a = lax.cond(on_low, lambda x: far_half(low_plane, x), lambda x: nothing(), blocks)
    b_next_high = go(after(b_own, low_a[0]), goal=back, takes_part=low_plane)
    out, high_a = lax.cond(
        on_low,
        lambda x, b, n, a: (shared(low_plane, b, n, *a), nothing()),
        lambda x, b, n, a: (jnp.zeros((2, 2, BS, BS), jnp.float32), far_half(high_plane, x)),
        blocks, b_own, b_next_low, low_a,
    )
    return lax.cond(
        on_low,
        lambda o, b, n, a: o,
        lambda o, b, n, a: shared(high_plane, b, n, *a),
        out, b_own, b_next_high, high_a,
    )


def solution(mesh):
    placed = (
        P("row", "col", None, None),
        P("row", "col"),
        P("row", "col"),
        P("row", "col", None, None),
        P("row", "col"),
        P("row", "col"),
        P("row", "col"),
    )
    return jax.shard_map(
        per_device,
        mesh=mesh,
        in_specs=placed,
        out_specs=P("row", "col", None, None),
        check_vma=False,
    )
```

```python
import functools

import jax
import jax.numpy as jnp
from jax import lax
from jax.experimental import pallas as pl
from jax.experimental.pallas import tpu as pltpu
from jax.sharding import PartitionSpec as P

BS = 128
VALUES = 4 * BS
ROWS = VALUES + 16
STEPS = 16.0
TOP = 32767.0
FLOOR = 2.0**-100


def level_of(biggest):
    return jnp.ceil(STEPS * jnp.log2(jnp.maximum(biggest, FLOOR))) + 1.0


def coded(values, level):
    scaled = values * (TOP * jnp.exp2(level * (-1.0 / STEPS)))
    return jnp.round(scaled).astype(jnp.int32).astype(jnp.int16)


def slot_sum(blocks, which, many, row, target):
    total = jnp.zeros((BS, BS), jnp.float32)
    live = many[0, row]
    for d in range(4):
        hit = jnp.logical_and(d < live, which[row, d] == target)
        total = total + blocks[row, d].astype(jnp.float32) * jnp.where(hit, 1.0, 0.0)
    return total


def level_rows(levels):
    at = lax.broadcasted_iota(jnp.int32, (16, BS), 0)
    rows = jnp.zeros((16, BS), jnp.float32)
    for n, level in enumerate(levels):
        rows = jnp.where(at == n, level, rows)
    return rows.astype(jnp.int32).astype(jnp.int16)


def pack_b(which, many, blocks, out):
    levels = []
    for k in range(2):
        sums = [slot_sum(blocks, which, many, k, j) for j in range(2)]
        biggest = jnp.max(jnp.maximum(jnp.abs(sums[0]), jnp.abs(sums[1])), axis=1, keepdims=True)
        level = level_of(biggest)
        for j in range(2):
            out[pl.ds((2 * k + j) * BS, BS), :] = coded(sums[j], level)
        levels.append(jnp.transpose(jnp.broadcast_to(level, (BS, BS)))[0:1, :])
    out[pl.ds(VALUES, 16), :] = level_rows(levels)


def pack_a(which, many, chip, blocks, own, sent):
    def one(first, out):
        levels = []
        for k in range(2):
            for i in range(2):
                total = slot_sum(blocks, which, many, first + k, i)
                level = level_of(jnp.max(jnp.abs(total), axis=0, keepdims=True))
                out[pl.ds((2 * k + i) * BS, BS), :] = coded(total, level)
                levels.append(level)
        out[pl.ds(VALUES, 16), :] = level_rows(levels)

    one(0, own)

    @pl.when(chip[0] < 4)
    def _():
        one(2, sent)

    @pl.when(chip[0] >= 4)
    def _():
        sent[...] = own[...]


SMEM = pl.BlockSpec(memory_space=pltpu.SMEM)
VMEM = pl.BlockSpec(memory_space=pltpu.VMEM)
PIECE = jax.ShapeDtypeStruct((ROWS, BS), jnp.int16)


def packed_b(blocks, which, many):
    return pl.pallas_call(
        pack_b,
        out_shape=PIECE,
        in_specs=[SMEM, SMEM, VMEM],
        out_specs=VMEM,
        name="pack_b",
        cost_estimate=pl.CostEstimate(flops=2_000_000, bytes_accessed=400_000, transcendentals=0),
    )(which, many, blocks)


def packed_a(blocks, which, many, chip):
    return pl.pallas_call(
        pack_a,
        out_shape=(PIECE,) * 2,
        in_specs=[SMEM, SMEM, SMEM, VMEM],
        out_specs=(VMEM,) * 2,
        name="pack_a",
        cost_estimate=pl.CostEstimate(flops=4_000_000, bytes_accessed=800_000, transcendentals=0),
    )(which, many, chip, blocks)


def two_parts(x):
    high = x.astype(jnp.bfloat16)
    return high, (x - high.astype(jnp.float32)).astype(jnp.bfloat16)


def section(a, b):
    a_levels = a[pl.ds(VALUES, 16), :].astype(jnp.int32).astype(jnp.float32)
    b_levels = b[pl.ds(VALUES, 16), :].astype(jnp.int32).astype(jnp.float32)
    a_scales = jnp.exp2(a_levels * (1.0 / STEPS))
    b_scales = jnp.exp2(b_levels * (1.0 / STEPS))
    lefts = []
    rights = []
    for k in range(2):
        tall = []
        wide = []
        for i in range(2):
            v = a[pl.ds((2 * k + i) * BS, BS), :].astype(jnp.int32).astype(jnp.float32)
            n = 2 * k + i
            tall.append((v * (1.0 / TOP)) * a_scales[n : n + 1, :] * b_scales[k : k + 1, :])
            wide.append(b[pl.ds(n * BS, BS), :].astype(jnp.int32).astype(jnp.float32))
        lefts.append(jnp.concatenate(tall, axis=0))
        rights.append(jnp.concatenate(wide, axis=1))
    a_high, a_low = two_parts(jnp.concatenate(lefts, axis=1))
    b_high, b_low = two_parts(jnp.concatenate(rights, axis=0))
    dot = functools.partial(jnp.dot, preferred_element_type=jnp.float32)
    return dot(a_high, b_high) + (dot(a_high, b_low) + dot(a_low, b_high))


def kept(keep, total, out):
    for i in range(2):
        for j in range(2):
            block = total[i * BS : (i + 1) * BS, j * BS : (j + 1) * BS] * (1.0 / TOP)
            out[i, j] = jnp.where(keep[i, j] == 1, block, 0.0)


def slots_of(spot):
    chip, core = spot[0], spot[1]
    return [lax.rem(chip + t, 4) for t in range(4)], [lax.rem(chip + core + t, 4) for t in range(4)]


def kept(keep, total, out):
    for i in range(2):
        for j in range(2):
            block = total[i * BS : (i + 1) * BS, j * BS : (j + 1) * BS] * (1.0 / TOP)
            out[i, j] = jnp.where(keep[i, j] == 1, block, 0.0)


def final(spot, keep, mine, others, b0, b1, b2, b3, c0, c1, c2, c3, out):
    total = jnp.zeros((2 * BS, 2 * BS), jnp.float32)
    for s, t, b, c in zip(*slots_of(spot), (b0, b1, b2, b3), (c0, c1, c2, c3)):
        total = total + section(mine.at[s], b) + section(others.at[t], c)
    kept(keep, total, out)


def summed(body, keep, *pieces):
    return pl.pallas_call(
        body,
        out_shape=jax.ShapeDtypeStruct((2, 2, BS, BS), jnp.float32),
        in_specs=[SMEM] * len(keep) + [VMEM] * len(pieces),
        out_specs=VMEM,
        name=body.__name__,
        cost_estimate=pl.CostEstimate(flops=800_000_000, bytes_accessed=2_500_000, transcendentals=0),
        compiler_params=pltpu.CompilerParams(vmem_limit_bytes=32 << 20),
    )(*keep, *pieces)


def moved(x, rows, cols, goal, takes_part=None):
    pairs = []
    for p in range(rows):
        for q in range(cols):
            if takes_part is None or takes_part(p, q):
                to_p, to_q = goal(p, q)
                pairs.append((p * cols + q, (to_p % rows) * cols + to_q % cols))
    return lax.ppermute(x, ("row", "col"), pairs)


def low_plane(p, q):
    return p % 2 == 0


def high_plane(p, q):
    return p % 2 == 1


def per_device(a_blocks, a_rows, a_count, b_blocks, b_cols, b_count, c_keep):
    rows = lax.axis_size("row")
    cols = lax.axis_size("col")
    go = functools.partial(moved, rows=rows, cols=cols)
    col_at = lax.axis_index("col")
    chip = col_at // 2
    core = col_at % 2

    on_low = lax.axis_index("row") % 2 == 0
    chip_at = chip.astype(jnp.int32).reshape(1)
    in_quad = chip % 4
    spot = jnp.stack([in_quad, core]).astype(jnp.int32)
    back = lambda p, q: (p - 1, q)

    def spread(x, t, plane):
        return go(x, goal=lambda p, q: (p - 2 * t, q), takes_part=plane)

    def after(x, done):
        return lax.optimization_barrier((x, done))[0]

    slot = lax.broadcasted_iota(jnp.int32, (4, 1, 1), 0)
    quads = [[8 * h + 2 * j + c for j in range(4)] for h in range(cols // 8) for c in range(2)]

    def own_spread(plane, b_own):
        def by_core(at):
            part = lambda p, q: plane(p, q) and q % 2 == at
            return lambda b: tuple(spread(b, t, part) for t in (1, 2, 3))

        return lax.cond(core == 0, by_core(0), by_core(1), b_own)

    def packed(b_own):
        return packed_a(after(a_blocks, b_own), a_rows, a_count.T, chip_at)

    def first_steps(plane, b_own, a_own, a_sent):
        a_far = go(a_sent, goal=lambda p, q: (p, q ^ 8), takes_part=plane)
        b_same = own_spread(plane, after(b_own, a_own))
        return (jnp.where(slot <= in_quad, a_own[None], a_far[None]), a_far, *b_same)

    def last_steps(plane, b_own, b_next, sets):
        offered, a_far, *b_same = sets
        mine = lax.all_to_all(offered, "col", 0, 0, axis_index_groups=quads)
        b_other = [spread(b_next, t, plane) for t in (1, 2, 3)]
        own_slot = jnp.logical_and(slot == in_quad, core == 0)
        given = jnp.where(own_slot, a_far[None], after(mine, b_other))
        others = go(given, goal=lambda p, q: (p, q ^ 1), takes_part=plane)
        out = summed(final, [spot, c_keep], mine, others, b_own, *b_same, b_next, *b_other)
        return out, others, b_other

    def blank():
        return jnp.zeros(PIECE.shape, PIECE.dtype)

    def open_low(b_own):
        return first_steps(low_plane, b_own, *packed(b_own))

    def open_high(b_own):
        return (jnp.zeros((4, *PIECE.shape), PIECE.dtype), blank(), *packed(b_own), blank())

    def close_low(b_own, b_next, sets):
        out, others, b_other = last_steps(low_plane, b_own, b_next, sets)
        return (out, others, blank(), *b_other)

    def middle_high(b_own, b_next, sets):
        empty = jnp.zeros((2, 2, BS, BS), jnp.float32)
        return (empty, *first_steps(high_plane, b_own, sets[2], sets[3]))

    b_own = packed_b(b_blocks, b_cols, b_count.T)
    b_next_low = go(b_own, goal=back, takes_part=high_plane)
    sets_low = lax.cond(on_low, open_low, open_high, b_own)
    b_next_high = go(after(b_own, sets_low[0]), goal=back, takes_part=low_plane)
    out, *sets_high = lax.cond(on_low, close_low, middle_high, b_own, b_next_low, sets_low)
    return lax.cond(
        on_low,
        lambda o, b, n, sets: o,
        lambda o, b, n, sets: last_steps(high_plane, b, n, sets)[0],
        out, b_own, b_next_high, sets_high,
    )


def solution(mesh):
    placed = (
        P("row", "col", None, None),
        P("row", "col"),
        P("row", "col"),
        P("row", "col", None, None),
        P("row", "col"),
        P("row", "col"),
        P("row", "col"),
    )
    return jax.shard_map(
        per_device,
        mesh=mesh,
        in_specs=placed,
        out_specs=P("row", "col", None, None),
        check_vma=False,
    )
```

```python
import functools

import jax
import jax.numpy as jnp
from jax import lax
from jax.experimental import pallas as pl
from jax.experimental.pallas import tpu as pltpu
from jax.sharding import PartitionSpec as P

BS = 128
VALUES = 4 * BS
ROWS = VALUES + 16
STEPS = 16.0
TOP = 32767.0
FLOOR = 2.0**-100


def level_of(biggest):
    return jnp.ceil(STEPS * jnp.log2(jnp.maximum(biggest, FLOOR))) + 1.0


def coded(values, level):
    scaled = values * (TOP * jnp.exp2(level * (-1.0 / STEPS)))
    return jnp.round(scaled).astype(jnp.int32).astype(jnp.int16)


def slot_sum(blocks, which, many, row, target):
    total = jnp.zeros((BS, BS), jnp.float32)
    live = many[0, row]
    for d in range(4):
        hit = jnp.logical_and(d < live, which[row, d] == target)
        total = total + blocks[row, d].astype(jnp.float32) * jnp.where(hit, 1.0, 0.0)
    return total


def level_rows(levels):
    at = lax.broadcasted_iota(jnp.int32, (16, BS), 0)
    rows = jnp.zeros((16, BS), jnp.float32)
    for n, level in enumerate(levels):
        rows = jnp.where(at == n, level, rows)
    return rows.astype(jnp.int32).astype(jnp.int16)


def pack_b(which, many, blocks, out):
    levels = []
    for k in range(2):
        sums = [slot_sum(blocks, which, many, k, j) for j in range(2)]
        biggest = jnp.max(jnp.maximum(jnp.abs(sums[0]), jnp.abs(sums[1])), axis=1, keepdims=True)
        level = level_of(biggest)
        for j in range(2):
            out[pl.ds((2 * k + j) * BS, BS), :] = coded(sums[j], level)
        levels.append(jnp.transpose(jnp.broadcast_to(level, (BS, BS)))[0:1, :])
    out[pl.ds(VALUES, 16), :] = level_rows(levels)


def pack_a(which, many, chip, blocks, own, sent):
    def one(first, out):
        levels = []
        for k in range(2):
            for i in range(2):
                total = slot_sum(blocks, which, many, first + k, i)
                level = level_of(jnp.max(jnp.abs(total), axis=0, keepdims=True))
                out[pl.ds((2 * k + i) * BS, BS), :] = coded(total, level)
                levels.append(level)
        out[pl.ds(VALUES, 16), :] = level_rows(levels)

    one(0, own)

    @pl.when(chip[0] < 4)
    def _():
        one(2, sent)

    @pl.when(chip[0] >= 4)
    def _():
        sent[...] = own[...]


SMEM = pl.BlockSpec(memory_space=pltpu.SMEM)
VMEM = pl.BlockSpec(memory_space=pltpu.VMEM)
PIECE = jax.ShapeDtypeStruct((ROWS, BS), jnp.int16)


def packed_b(blocks, which, many):
    return pl.pallas_call(
        pack_b,
        out_shape=PIECE,
        in_specs=[SMEM, SMEM, VMEM],
        out_specs=VMEM,
        name="pack_b",
        cost_estimate=pl.CostEstimate(flops=2_000_000, bytes_accessed=400_000, transcendentals=0),
    )(which, many, blocks)


def packed_a(blocks, which, many, chip):
    return pl.pallas_call(
        pack_a,
        out_shape=(PIECE,) * 2,
        in_specs=[SMEM, SMEM, SMEM, VMEM],
        out_specs=(VMEM,) * 2,
        name="pack_a",
        cost_estimate=pl.CostEstimate(flops=4_000_000, bytes_accessed=800_000, transcendentals=0),
    )(which, many, chip, blocks)


def two_parts(x):
    high = x.astype(jnp.bfloat16)
    return high, (x - high.astype(jnp.float32)).astype(jnp.bfloat16)


def section(a, b):
    a_levels = a[pl.ds(VALUES, 16), :].astype(jnp.int32).astype(jnp.float32)
    b_levels = b[pl.ds(VALUES, 16), :].astype(jnp.int32).astype(jnp.float32)
    a_scales = jnp.exp2(a_levels * (1.0 / STEPS))
    b_scales = jnp.exp2(b_levels * (1.0 / STEPS))
    lefts = []
    rights = []
    for k in range(2):
        tall = []
        wide = []
        for i in range(2):
            v = a[pl.ds((2 * k + i) * BS, BS), :].astype(jnp.int32).astype(jnp.float32)
            n = 2 * k + i
            tall.append((v * (1.0 / TOP)) * a_scales[n : n + 1, :] * b_scales[k : k + 1, :])
            wide.append(b[pl.ds(n * BS, BS), :].astype(jnp.int32).astype(jnp.float32))
        lefts.append(jnp.concatenate(tall, axis=0))
        rights.append(jnp.concatenate(wide, axis=1))
    a_high, a_low = two_parts(jnp.concatenate(lefts, axis=1))
    b_high, b_low = two_parts(jnp.concatenate(rights, axis=0))
    dot = functools.partial(jnp.dot, preferred_element_type=jnp.float32)
    return dot(a_high, b_high) + (dot(a_high, b_low) + dot(a_low, b_high))


def kept(keep, total, out):
    for i in range(2):
        for j in range(2):
            block = total[i * BS : (i + 1) * BS, j * BS : (j + 1) * BS] * (1.0 / TOP)
            out[i, j] = jnp.where(keep[i, j] == 1, block, 0.0)


def slots_of(spot):
    chip, core = spot[0], spot[1]
    return [lax.rem(chip + t, 4) for t in range(4)], [lax.rem(chip + core + t, 4) for t in range(4)]


def kept(keep, total, out):
    for i in range(2):
        for j in range(2):
            block = total[i * BS : (i + 1) * BS, j * BS : (j + 1) * BS] * (1.0 / TOP)
            out[i, j] = jnp.where(keep[i, j] == 1, block, 0.0)


def even(spot, mine, b0, b1, b2, b3, out):
    total = jnp.zeros((2 * BS, 2 * BS), jnp.float32)
    for s, b in zip(slots_of(spot)[0], (b0, b1, b2, b3)):
        total = total + section(mine.at[s], b)
    for i in range(2):
        for j in range(2):
            out[i, j] = total[i * BS : (i + 1) * BS, j * BS : (j + 1) * BS]


def odd(spot, keep, begun, others, c0, c1, c2, c3, out):
    total = jnp.concatenate([jnp.concatenate([begun[i, 0], begun[i, 1]], axis=1) for i in range(2)], axis=0)
    for t, c in zip(slots_of(spot)[1], (c0, c1, c2, c3)):
        total = total + section(others.at[t], c)
    kept(keep, total, out)


def summed(body, keep, *pieces):
    return pl.pallas_call(
        body,
        out_shape=jax.ShapeDtypeStruct((2, 2, BS, BS), jnp.float32),
        in_specs=[SMEM] * len(keep) + [VMEM] * len(pieces),
        out_specs=VMEM,
        name=body.__name__,
        cost_estimate=pl.CostEstimate(flops=800_000_000, bytes_accessed=2_500_000, transcendentals=0),
        compiler_params=pltpu.CompilerParams(vmem_limit_bytes=32 << 20),
    )(*keep, *pieces)


def moved(x, rows, cols, goal, takes_part=None):
    pairs = []
    for p in range(rows):
        for q in range(cols):
            if takes_part is None or takes_part(p, q):
                to_p, to_q = goal(p, q)
                pairs.append((p * cols + q, (to_p % rows) * cols + to_q % cols))
    return lax.ppermute(x, ("row", "col"), pairs)


def low_plane(p, q):
    return p % 2 == 0


def high_plane(p, q):
    return p % 2 == 1


def per_device(a_blocks, a_rows, a_count, b_blocks, b_cols, b_count, c_keep):
    rows = lax.axis_size("row")
    cols = lax.axis_size("col")
    go = functools.partial(moved, rows=rows, cols=cols)
    col_at = lax.axis_index("col")
    chip = col_at // 2
    core = col_at % 2

    on_low = lax.axis_index("row") % 2 == 0
    chip_at = chip.astype(jnp.int32).reshape(1)
    in_quad = chip % 4
    spot = jnp.stack([in_quad, core]).astype(jnp.int32)
    back = lambda p, q: (p - 1, q)

    def spread(x, t, plane):
        return go(x, goal=lambda p, q: (p - 2 * t, q), takes_part=plane)

    def after(x, done):
        return lax.optimization_barrier((x, done))[0]

    slot = lax.broadcasted_iota(jnp.int32, (4, 1, 1), 0)
    quads = [[8 * h + 2 * j + c for j in range(4)] for h in range(cols // 8) for c in range(2)]

    def own_spread(plane, b_own, steps):
        def by_core(at):
            part = lambda p, q: plane(p, q) and q % 2 == at
            return lambda b: tuple(spread(b, t, part) for t in steps)

        return lax.cond(core == 0, by_core(0), by_core(1), b_own)

    def packed(b_own):
        return packed_a(after(a_blocks, b_own), a_rows, a_count.T, chip_at)

    def first_steps(plane, b_own, a_own, a_sent, steps):
        a_far = go(a_sent, goal=lambda p, q: (p, q ^ 8), takes_part=plane)
        return (a_far, *own_spread(plane, after(b_own, a_own), steps))

    def offered(a_own, a_far):
        return jnp.where(slot <= in_quad, a_own[None], a_far[None])

    def last_steps(plane, b_own, b_next, offer, a_far, b_same):
        mine = lax.all_to_all(offer, "col", 0, 0, axis_index_groups=quads)
        b_other = [spread(b_next, t, plane) for t in (1, 2, 3)]
        own_slot = jnp.logical_and(slot == in_quad, core == 0)
        given = jnp.where(own_slot, a_far[None], after(mine, b_other))
        others = go(given, goal=lambda p, q: (p, q ^ 1), takes_part=plane)
        begun = summed(even, [spot], mine, b_own, *b_same)
        out = summed(odd, [spot, c_keep], begun, others, b_next, *b_other)
        return out, others, b_other

    def blank():
        return jnp.zeros(PIECE.shape, PIECE.dtype)

    def open_low(b_own):
        a_own, a_sent = packed(b_own)
        return (a_own, *first_steps(low_plane, b_own, a_own, a_sent, (1, 2, 3)))

    def open_high(b_own):
        a_own, a_sent = packed(b_own)
        return (a_own, a_sent, blank(), blank(), blank())

    def close_low(b_own, b_next, sets):
        a_own, a_far, *b_same = sets
        offer = offered(a_own, a_far)
        out, others, b_other = last_steps(low_plane, b_own, b_next, offer, a_far, b_same)
        return (out, others, blank(), *b_other)

    def middle_high(b_own, b_next, sets):
        empty = jnp.zeros((2, 2, BS, BS), jnp.float32)
        a_own, a_sent = sets[:2]
        a_far, *b_same = first_steps(high_plane, b_own, a_own, a_sent, (1, 2, 3))
        return (empty, offered(a_own, a_far), a_far, *b_same)

    b_own = packed_b(b_blocks, b_cols, b_count.T)
    b_next_low = go(b_own, goal=back, takes_part=high_plane)
    sets_low = lax.cond(on_low, open_low, open_high, b_own)
    b_next_high = go(after(b_own, sets_low[0]), goal=back, takes_part=low_plane)
    out, *sets_high = lax.cond(on_low, close_low, middle_high, b_own, b_next_low, sets_low)
    return lax.cond(
        on_low,
        lambda o, b, n, sets: o,
        lambda o, b, n, sets: last_steps(high_plane, b, n, sets[0], sets[1], sets[2:])[0],
        out, b_own, b_next_high, sets_high,
    )


def solution(mesh):
    placed = (
        P("row", "col", None, None),
        P("row", "col"),
        P("row", "col"),
        P("row", "col", None, None),
        P("row", "col"),
        P("row", "col"),
        P("row", "col"),
    )
    return jax.shard_map(
        per_device,
        mesh=mesh,
        in_specs=placed,
        out_specs=P("row", "col", None, None),
        check_vma=False,
    )
```

```python
import functools

import jax
import jax.numpy as jnp
from jax import lax
from jax.experimental import pallas as pl
from jax.experimental.pallas import tpu as pltpu
from jax.sharding import PartitionSpec as P

BS = 128
VALUES = 4 * BS
ROWS = VALUES + 16
STEPS = 16.0
TOP = 32767.0
FLOOR = 2.0**-100


def level_of(biggest):
    return jnp.ceil(STEPS * jnp.log2(jnp.maximum(biggest, FLOOR))) + 1.0


def coded(values, level):
    scaled = values * (TOP * jnp.exp2(level * (-1.0 / STEPS)))
    return jnp.round(scaled).astype(jnp.int32).astype(jnp.int16)


def slot_sum(blocks, which, many, row, target):
    total = jnp.zeros((BS, BS), jnp.float32)
    live = many[0, row]
    for d in range(4):
        hit = jnp.logical_and(d < live, which[row, d] == target)
        total = total + blocks[row, d].astype(jnp.float32) * jnp.where(hit, 1.0, 0.0)
    return total


def level_rows(levels):
    at = lax.broadcasted_iota(jnp.int32, (16, BS), 0)
    rows = jnp.zeros((16, BS), jnp.float32)
    for n, level in enumerate(levels):
        rows = jnp.where(at == n, level, rows)
    return rows.astype(jnp.int32).astype(jnp.int16)


def pack_b(which, many, blocks, out):
    levels = []
    for k in range(2):
        sums = [slot_sum(blocks, which, many, k, j) for j in range(2)]
        biggest = jnp.max(jnp.maximum(jnp.abs(sums[0]), jnp.abs(sums[1])), axis=1, keepdims=True)
        level = level_of(biggest)
        for j in range(2):
            out[pl.ds((2 * k + j) * BS, BS), :] = coded(sums[j], level)
        levels.append(jnp.transpose(jnp.broadcast_to(level, (BS, BS)))[0:1, :])
    out[pl.ds(VALUES, 16), :] = level_rows(levels)


def pack_a(which, many, chip, blocks, own, sent):
    def one(first, out):
        levels = []
        for k in range(2):
            for i in range(2):
                total = slot_sum(blocks, which, many, first + k, i)
                level = level_of(jnp.max(jnp.abs(total), axis=0, keepdims=True))
                out[pl.ds((2 * k + i) * BS, BS), :] = coded(total, level)
                levels.append(level)
        out[pl.ds(VALUES, 16), :] = level_rows(levels)

    one(0, own)

    @pl.when(chip[0] < 4)
    def _():
        one(2, sent)

    @pl.when(chip[0] >= 4)
    def _():
        sent[...] = own[...]


SMEM = pl.BlockSpec(memory_space=pltpu.SMEM)
VMEM = pl.BlockSpec(memory_space=pltpu.VMEM)
PIECE = jax.ShapeDtypeStruct((ROWS, BS), jnp.int16)


def pack_all(b_which, b_many, a_which, a_many, chip, b_blocks, a_blocks, b_own, a_own, a_sent):
    pack_b(b_which, b_many, b_blocks, b_own)
    pack_a(a_which, a_many, chip, a_blocks, a_own, a_sent)


def packed(*inputs):
    return pl.pallas_call(
        pack_all,
        out_shape=(PIECE,) * 3,
        in_specs=[SMEM] * 5 + [VMEM] * 2,
        out_specs=(VMEM,) * 3,
        name="pack_all",
        cost_estimate=pl.CostEstimate(flops=6_000_000, bytes_accessed=1_200_000, transcendentals=0),
    )(*inputs)


def two_parts(x):
    high = x.astype(jnp.bfloat16)
    return high, (x - high.astype(jnp.float32)).astype(jnp.bfloat16)


def section(a, b):
    a_levels = a[pl.ds(VALUES, 16), :].astype(jnp.int32).astype(jnp.float32)
    b_levels = b[pl.ds(VALUES, 16), :].astype(jnp.int32).astype(jnp.float32)
    a_scales = jnp.exp2(a_levels * (1.0 / STEPS))
    b_scales = jnp.exp2(b_levels * (1.0 / STEPS))
    lefts = []
    rights = []
    for k in range(2):
        tall = []
        wide = []
        for i in range(2):
            v = a[pl.ds((2 * k + i) * BS, BS), :].astype(jnp.int32).astype(jnp.float32)
            n = 2 * k + i
            tall.append((v * (1.0 / TOP)) * a_scales[n : n + 1, :] * b_scales[k : k + 1, :])
            wide.append(b[pl.ds(n * BS, BS), :].astype(jnp.int32).astype(jnp.float32))
        lefts.append(jnp.concatenate(tall, axis=0))
        rights.append(jnp.concatenate(wide, axis=1))
    a_high, a_low = two_parts(jnp.concatenate(lefts, axis=1))
    b_high, b_low = two_parts(jnp.concatenate(rights, axis=0))
    dot = functools.partial(jnp.dot, preferred_element_type=jnp.float32)
    return dot(a_high, b_high) + (dot(a_high, b_low) + dot(a_low, b_high))


def kept(keep, total, out):
    for i in range(2):
        for j in range(2):
            block = total[i * BS : (i + 1) * BS, j * BS : (j + 1) * BS] * (1.0 / TOP)
            out[i, j] = jnp.where(keep[i, j] == 1, block, 0.0)


def slots_of(spot):
    chip, core = spot[0], spot[1]
    return [lax.rem(chip + t, 4) for t in range(4)], [lax.rem(chip + core + t, 4) for t in range(4)]


def kept(keep, total, out):
    for i in range(2):
        for j in range(2):
            block = total[i * BS : (i + 1) * BS, j * BS : (j + 1) * BS] * (1.0 / TOP)
            out[i, j] = jnp.where(keep[i, j] == 1, block, 0.0)


def even(spot, mine, b0, b1, b2, b3, out):
    total = jnp.zeros((2 * BS, 2 * BS), jnp.float32)
    for s, b in zip(slots_of(spot)[0], (b0, b1, b2, b3)):
        total = total + section(mine.at[s], b)
    for i in range(2):
        for j in range(2):
            out[i, j] = total[i * BS : (i + 1) * BS, j * BS : (j + 1) * BS]


def odd(spot, keep, begun, others, c0, c1, c2, c3, out):
    total = jnp.concatenate([jnp.concatenate([begun[i, 0], begun[i, 1]], axis=1) for i in range(2)], axis=0)
    for t, c in zip(slots_of(spot)[1], (c0, c1, c2, c3)):
        total = total + section(others.at[t], c)
    kept(keep, total, out)


def summed(body, keep, *pieces):
    return pl.pallas_call(
        body,
        out_shape=jax.ShapeDtypeStruct((2, 2, BS, BS), jnp.float32),
        in_specs=[SMEM] * len(keep) + [VMEM] * len(pieces),
        out_specs=VMEM,
        name=body.__name__,
        cost_estimate=pl.CostEstimate(flops=800_000_000, bytes_accessed=2_500_000, transcendentals=0),
        compiler_params=pltpu.CompilerParams(vmem_limit_bytes=32 << 20),
    )(*keep, *pieces)


def moved(x, rows, cols, goal, takes_part=None):
    pairs = []
    for p in range(rows):
        for q in range(cols):
            if takes_part is None or takes_part(p, q):
                to_p, to_q = goal(p, q)
                pairs.append((p * cols + q, (to_p % rows) * cols + to_q % cols))
    return lax.ppermute(x, ("row", "col"), pairs)


def low_plane(p, q):
    return p % 2 == 0


def high_plane(p, q):
    return p % 2 == 1


def per_device(a_blocks, a_rows, a_count, b_blocks, b_cols, b_count, c_keep):
    rows = lax.axis_size("row")
    cols = lax.axis_size("col")
    go = functools.partial(moved, rows=rows, cols=cols)
    col_at = lax.axis_index("col")
    chip = col_at // 2
    core = col_at % 2

    on_low = lax.axis_index("row") % 2 == 0
    chip_at = chip.astype(jnp.int32).reshape(1)
    in_quad = chip % 4
    spot = jnp.stack([in_quad, core]).astype(jnp.int32)
    back = lambda p, q: (p - 1, q)

    def spread(x, t, plane):
        return go(x, goal=lambda p, q: (p - 2 * t, q), takes_part=plane)

    def after(x, done):
        return lax.optimization_barrier((x, done))[0]

    slot = lax.broadcasted_iota(jnp.int32, (4, 1, 1), 0)
    quads = [[8 * h + 2 * j + c for j in range(4)] for h in range(cols // 8) for c in range(2)]

    def own_spread(plane, b_own, steps):
        def by_core(at):
            part = lambda p, q: plane(p, q) and q % 2 == at
            return lambda b: tuple(spread(b, t, part) for t in steps)

        return lax.cond(core == 0, by_core(0), by_core(1), b_own)

    def first_steps(plane, b_own, a_own, a_sent, steps):
        a_far = go(a_sent, goal=lambda p, q: (p, q ^ 8), takes_part=plane)
        return (a_far, *own_spread(plane, after(b_own, a_own), steps))

    def offered(a_own, a_far):
        return jnp.where(slot <= in_quad, a_own[None], a_far[None])

    def last_steps(plane, b_own, b_next, offer, a_far, b_same, fills):
        mine = lax.all_to_all(offer, "col", 0, 0, axis_index_groups=quads)
        b_other = [spread(b_next, t, plane) for t in (1, 2, 3)]
        own_slot = jnp.logical_and(slot == in_quad, core == 0)
        filler = b_other[0] ^ 1 if fills else b_other[0]
        given = jnp.where(own_slot, a_far[None], after(mine, (b_other, filler)))
        others = go(given, goal=lambda p, q: (p, q ^ 1), takes_part=plane)
        begun = summed(even, [spot], mine, b_own, *b_same)
        out = summed(odd, [spot, c_keep], begun, others, b_next, *b_other)
        return out, others, b_other, filler

    def blank():
        return jnp.zeros(PIECE.shape, PIECE.dtype)

    def open_low(b_own, a_own, a_sent):
        return first_steps(low_plane, b_own, a_own, a_sent, (1, 2, 3))

    def open_high(b_own, a_own, a_sent):
        return tuple(blank() for _ in range(4))

    def close_low(b_own, b_next, a_own, a_sent, sets):
        a_far, *b_same = sets
        offer = offered(a_own, a_far)
        out, others, b_other, filler = last_steps(low_plane, b_own, b_next, offer, a_far, b_same, True)
        return (out, others, filler, *b_other)

    def middle_high(b_own, b_next, a_own, a_sent, sets):
        empty = jnp.zeros((2, 2, BS, BS), jnp.float32)
        a_far, *b_same = first_steps(high_plane, b_own, a_own, a_sent, (1, 2, 3))
        return (empty, offered(a_own, a_far), a_far, *b_same)

    b_own, a_own, a_sent = packed(b_cols, b_count.T, a_rows, a_count.T, chip_at, b_blocks, a_blocks)
    b_next_low = go(b_own, goal=back, takes_part=high_plane)
    sets_low = lax.cond(on_low, open_low, open_high, b_own, a_own, a_sent)
    b_next_high = go(after(b_own, sets_low[0]), goal=back, takes_part=low_plane)
    out, *sets_high = lax.cond(on_low, close_low, middle_high, b_own, b_next_low, a_own, a_sent, sets_low)
    return lax.cond(
        on_low,
        lambda o, b, n, sets: o,
        lambda o, b, n, sets: last_steps(high_plane, b, n, sets[0], sets[1], sets[2:], False)[0],
        out, b_own, b_next_high, sets_high,
    )


def solution(mesh):
    placed = (
        P("row", "col", None, None),
        P("row", "col"),
        P("row", "col"),
        P("row", "col", None, None),
        P("row", "col"),
        P("row", "col"),
        P("row", "col"),
    )
    return jax.shard_map(
        per_device,
        mesh=mesh,
        in_specs=placed,
        out_specs=P("row", "col", None, None),
        check_vma=False,
    )
```

```python
import functools

import jax
import jax.numpy as jnp
from jax import lax
from jax.experimental import pallas as pl
from jax.experimental.pallas import tpu as pltpu
from jax.sharding import PartitionSpec as P

BS = 128
VALUES = 4 * BS
ROWS = VALUES + 16
STEPS = 16.0
TOP = 32767.0
FLOOR = 2.0**-100


def level_of(biggest):
    return jnp.ceil(STEPS * jnp.log2(jnp.maximum(biggest, FLOOR))) + 1.0


def coded(values, level):
    scaled = values * (TOP * jnp.exp2(level * (-1.0 / STEPS)))
    return jnp.round(scaled).astype(jnp.int32).astype(jnp.int16)


def slot_sum(blocks, which, many, row, target):
    total = jnp.zeros((BS, BS), jnp.float32)
    live = many[0, row]
    for d in range(4):
        hit = jnp.logical_and(d < live, which[row, d] == target)
        total = total + blocks[row, d].astype(jnp.float32) * jnp.where(hit, 1.0, 0.0)
    return total


def level_rows(levels):
    at = lax.broadcasted_iota(jnp.int32, (16, BS), 0)
    rows = jnp.zeros((16, BS), jnp.float32)
    for n, level in enumerate(levels):
        rows = jnp.where(at == n, level, rows)
    return rows.astype(jnp.int32).astype(jnp.int16)


def pack_b(which, many, blocks, out):
    levels = []
    for k in range(2):
        sums = [slot_sum(blocks, which, many, k, j) for j in range(2)]
        biggest = jnp.max(jnp.maximum(jnp.abs(sums[0]), jnp.abs(sums[1])), axis=1, keepdims=True)
        level = level_of(biggest)
        for j in range(2):
            out[pl.ds((2 * k + j) * BS, BS), :] = coded(sums[j], level)
        levels.append(jnp.transpose(jnp.broadcast_to(level, (BS, BS)))[0:1, :])
    out[pl.ds(VALUES, 16), :] = level_rows(levels)


def pack_a(which, many, chip, blocks, own, sent):
    def one(first, out):
        levels = []
        for k in range(2):
            for i in range(2):
                total = slot_sum(blocks, which, many, first + k, i)
                level = level_of(jnp.max(jnp.abs(total), axis=0, keepdims=True))
                out[pl.ds((2 * k + i) * BS, BS), :] = coded(total, level)
                levels.append(level)
        out[pl.ds(VALUES, 16), :] = level_rows(levels)

    one(0, own)

    @pl.when(chip[0] < 4)
    def _():
        one(2, sent)

    @pl.when(chip[0] >= 4)
    def _():
        sent[...] = own[...]


SMEM = pl.BlockSpec(memory_space=pltpu.SMEM)
VMEM = pl.BlockSpec(memory_space=pltpu.VMEM)
PIECE = jax.ShapeDtypeStruct((ROWS, BS), jnp.int16)


def pack_all(b_which, b_many, a_which, a_many, chip, b_blocks, a_blocks, b_own, a_own, a_sent):
    pack_b(b_which, b_many, b_blocks, b_own)
    pack_a(a_which, a_many, chip, a_blocks, a_own, a_sent)


def packed(*inputs):
    return pl.pallas_call(
        pack_all,
        out_shape=(PIECE,) * 3,
        in_specs=[SMEM] * 5 + [VMEM] * 2,
        out_specs=(VMEM,) * 3,
        name="pack_all",
        cost_estimate=pl.CostEstimate(flops=6_000_000, bytes_accessed=1_200_000, transcendentals=0),
    )(*inputs)


def two_parts(x):
    high = x.astype(jnp.bfloat16)
    return high, (x - high.astype(jnp.float32)).astype(jnp.bfloat16)


def section(a, b):
    a_levels = a[pl.ds(VALUES, 16), :].astype(jnp.int32).astype(jnp.float32)
    b_levels = b[pl.ds(VALUES, 16), :].astype(jnp.int32).astype(jnp.float32)
    a_scales = jnp.exp2(a_levels * (1.0 / STEPS))
    b_scales = jnp.exp2(b_levels * (1.0 / STEPS))
    lefts = []
    rights = []
    for k in range(2):
        tall = []
        wide = []
        for i in range(2):
            v = a[pl.ds((2 * k + i) * BS, BS), :].astype(jnp.int32).astype(jnp.float32)
            n = 2 * k + i
            tall.append((v * (1.0 / TOP)) * a_scales[n : n + 1, :] * b_scales[k : k + 1, :])
            wide.append(b[pl.ds(n * BS, BS), :].astype(jnp.int32).astype(jnp.float32))
        lefts.append(jnp.concatenate(tall, axis=0))
        rights.append(jnp.concatenate(wide, axis=1))
    a_high, a_low = two_parts(jnp.concatenate(lefts, axis=1))
    b_high, b_low = two_parts(jnp.concatenate(rights, axis=0))
    dot = functools.partial(jnp.dot, preferred_element_type=jnp.float32)
    return dot(a_high, b_high) + (dot(a_high, b_low) + dot(a_low, b_high))


def kept(keep, total, out):
    for i in range(2):
        for j in range(2):
            block = total[i * BS : (i + 1) * BS, j * BS : (j + 1) * BS] * (1.0 / TOP)
            out[i, j] = jnp.where(keep[i, j] == 1, block, 0.0)


def slots_of(spot):
    chip, core = spot[0], spot[1]
    return [lax.rem(chip + t, 4) for t in range(4)], [lax.rem(chip + core + t, 4) for t in range(4)]


def kept(keep, total, out):
    for i in range(2):
        for j in range(2):
            block = total[i * BS : (i + 1) * BS, j * BS : (j + 1) * BS] * (1.0 / TOP)
            out[i, j] = jnp.where(keep[i, j] == 1, block, 0.0)


def even(spot, mine, b0, b1, b2, b3, out):
    total = jnp.zeros((2 * BS, 2 * BS), jnp.float32)
    for s, b in zip(slots_of(spot)[0], (b0, b1, b2, b3)):
        total = total + section(mine.at[s], b)
    for i in range(2):
        for j in range(2):
            out[i, j] = total[i * BS : (i + 1) * BS, j * BS : (j + 1) * BS]


def odd(spot, keep, begun, others, c0, c1, c2, c3, out):
    total = jnp.concatenate([jnp.concatenate([begun[i, 0], begun[i, 1]], axis=1) for i in range(2)], axis=0)
    for t, c in zip(slots_of(spot)[1], (c0, c1, c2, c3)):
        total = total + section(others.at[t], c)
    kept(keep, total, out)


def summed(body, keep, *pieces):
    return pl.pallas_call(
        body,
        out_shape=jax.ShapeDtypeStruct((2, 2, BS, BS), jnp.float32),
        in_specs=[SMEM] * len(keep) + [VMEM] * len(pieces),
        out_specs=VMEM,
        name=body.__name__,
        cost_estimate=pl.CostEstimate(flops=800_000_000, bytes_accessed=2_500_000, transcendentals=0),
        compiler_params=pltpu.CompilerParams(vmem_limit_bytes=32 << 20),
    )(*keep, *pieces)


def moved(x, rows, cols, goal, takes_part=None):
    pairs = []
    for p in range(rows):
        for q in range(cols):
            if takes_part is None or takes_part(p, q):
                to_p, to_q = goal(p, q)
                pairs.append((p * cols + q, (to_p % rows) * cols + to_q % cols))
    return lax.ppermute(x, ("row", "col"), pairs)


def low_plane(p, q):
    return p % 2 == 0


def high_plane(p, q):
    return p % 2 == 1


def per_device(a_blocks, a_rows, a_count, b_blocks, b_cols, b_count, c_keep):
    rows = lax.axis_size("row")
    cols = lax.axis_size("col")
    go = functools.partial(moved, rows=rows, cols=cols)
    col_at = lax.axis_index("col")
    chip = col_at // 2
    core = col_at % 2

    on_low = lax.axis_index("row") % 2 == 0
    chip_at = chip.astype(jnp.int32).reshape(1)
    in_quad = chip % 4
    spot = jnp.stack([in_quad, core]).astype(jnp.int32)
    back = lambda p, q: (p - 1, q)

    def spread(x, t, plane):
        return go(x, goal=lambda p, q: (p - 2 * t, q), takes_part=plane)

    def after(x, done):
        return lax.optimization_barrier((x, done))[0]

    slot = lax.broadcasted_iota(jnp.int32, (4, 1, 1), 0)
    quads = [[8 * h + 2 * j + c for j in range(4)] for h in range(cols // 8) for c in range(2)]

    def own_spread(plane, b_own, steps):
        def by_core(at):
            part = lambda p, q: plane(p, q) and q % 2 == at
            return lambda b: tuple(spread(b, t, part) for t in steps)

        return lax.cond(core == 0, by_core(0), by_core(1), b_own)

    def first_steps(plane, b_own, a_own, a_sent, steps):
        a_far = go(a_sent, goal=lambda p, q: (p, q ^ 8), takes_part=plane)
        return (a_far, *own_spread(plane, after(b_own, a_own), steps))

    def offered(a_own, a_far):
        return jnp.where(slot <= in_quad, a_own[None], a_far[None])

    def last_steps(plane, b_own, b_next, offer, a_far, b_same, fills):
        mine = lax.all_to_all(offer, "col", 0, 0, axis_index_groups=quads)
        b_other = [spread(b_next, t, plane) for t in (1, 2, 3)]
        own_slot = jnp.logical_and(slot == in_quad, core == 0)
        filler = b_other[0] ^ 1 if fills else b_other[0]
        given = jnp.where(own_slot, a_far[None], after(mine, (b_other, filler)))
        others = go(given, goal=lambda p, q: (p, q ^ 1), takes_part=plane)
        begun = summed(even, [spot], mine, b_own, *b_same)
        out = summed(odd, [spot, c_keep], begun, others, b_next, *b_other)
        return out, others, b_other, filler

    def blank():
        return jnp.zeros(PIECE.shape, PIECE.dtype)

    def open_low(b_own, a_own, a_sent):
        a_far, *b_same = first_steps(low_plane, b_own, a_own, a_sent, (1, 2, 3))
        return (offered(a_own, a_far), a_far, *b_same)

    def open_high(b_own, a_own, a_sent):
        return (jnp.zeros((4, *PIECE.shape), PIECE.dtype), *[blank() for _ in range(4)])

    def close_low(b_own, b_next, a_own, a_sent, sets):
        offer, a_far, *b_same = sets
        out, others, b_other, filler = last_steps(low_plane, b_own, b_next, offer, a_far, b_same, True)
        return (out, others, filler, *b_other)

    def middle_high(b_own, b_next, a_own, a_sent, sets):
        empty = jnp.zeros((2, 2, BS, BS), jnp.float32)
        a_far, *b_same = first_steps(high_plane, b_own, a_own, a_sent, (1, 2, 3))
        return (empty, offered(a_own, a_far), a_far, *b_same)

    b_own, a_own, a_sent = packed(b_cols, b_count.T, a_rows, a_count.T, chip_at, b_blocks, a_blocks)
    b_next_low = go(b_own, goal=back, takes_part=high_plane)
    sets_low = lax.cond(on_low, open_low, open_high, b_own, a_own, a_sent)
    b_next_high = go(after(b_own, sets_low[0]), goal=back, takes_part=low_plane)
    out, *sets_high = lax.cond(on_low, close_low, middle_high, b_own, b_next_low, a_own, a_sent, sets_low)
    return lax.cond(
        on_low,
        lambda o, b, n, sets: o,
        lambda o, b, n, sets: last_steps(high_plane, b, n, sets[0], sets[1], sets[2:], False)[0],
        out, b_own, b_next_high, sets_high,
    )


def solution(mesh):
    placed = (
        P("row", "col", None, None),
        P("row", "col"),
        P("row", "col"),
        P("row", "col", None, None),
        P("row", "col"),
        P("row", "col"),
        P("row", "col"),
    )
    return jax.shard_map(
        per_device,
        mesh=mesh,
        in_specs=placed,
        out_specs=P("row", "col", None, None),
        check_vma=False,
    )
```
